512 devices in a mesh: row: 16 (over x_lo, y, core), col: 32 (over x_hi, z).
Axes of the slice: x: 4 (x_hi: 2, x_lo: 2; x = x_hi * 2 + x_lo), y: 4, z: 16, core: 2. Of those that a mesh axis runs over, the one named last changes fastest.
Arguments:
- seq_ids: int32 [1024], replicated, may hold values from 0 to 3, never falling along the last dimension, each value on 1 to 512 neighbouring positions
- query_inputs: bfloat16 [1024, 8192], P('col', 'row'), may hold values from -6 to 6
- query_grads: bfloat16 [1024, 8192], P('row', 'col'), may hold values from -0.25 to 0.25
- query_act_basis: bfloat16 [8192, 8192], P('row', 'col'), may hold values from -0.0625 to 0.0625
- query_grad_basis: bfloat16 [8192, 8192], P('col', 'row'), may hold values from -0.0625 to 0.0625
- output_inputs: bfloat16 [1024, 8192], P('col', 'row'), may hold values from -6 to 6
- output_grads: bfloat16 [1024, 8192], P('row', 'col'), may hold values from -0.25 to 0.25
- output_act_basis: bfloat16 [8192, 8192], P('row', 'col'), may hold values from -0.0625 to 0.0625
- output_grad_basis: bfloat16 [8192, 8192], P('col', 'row'), may hold values from -0.0625 to 0.0625
Outputs:
- query_corr: float32 [8192, 8192], P('row', 'col')
- output_corr: float32 [8192, 8192], P('row', 'col')
The draws below stay inside these ranges and needn't reach their ends.
Inputs may be any that keep to these rules, and one draw needn't show every extreme that they name: seq_ids never falls along the tokens; each of the 4 sequences holds 1 to 512 tokens, and one holds exactly 512.
All inputs are finite; a program needn't handle non-finite values.
Results may differ from the reference program's by a relative error of at most 0.0003.
Values may be sent and summed in bfloat16 or wider, within the bound.
No kernel may reach another device: no remote copies, remote signals or barrier semaphores. Data moves between devices by JAX's collectives and lax.ppermute only.
A program may use at most 64 MiB of HBM per device.

```python
import math
import jax
import jax.numpy as jnp
import numpy as np
from jax import lax

D = 8192
TOKENS = 1024
SEQS = 4
MOST = 512


def block_levels(key, extent, cuts, low, largest):
    factor_of, own = 1.0, jax.random.fold_in(key, 6)
    for position, parts in cuts:
        steps = jnp.exp(jax.random.uniform(jax.random.fold_in(own, position), (parts,), jnp.float32, low / len(cuts), largest / len(cuts)))
        factor_of = factor_of * jnp.repeat(steps, extent[position] // parts).reshape([-1 if axis == position else 1 for axis in range(len(extent))])
    return factor_of


def profile(count, total, bound, lean):
    portions = [(1 << 20) // math.isqrt(standing ** lean) + 1 for standing in range(2, count + 1)]
    spare, given = total - bound - (count - 1), [1] * (count - 1)
    while spare > 0:
        free = [i for i in range(count - 1) if given[i] < bound]
        pool, budget = sum([portions[i] for i in free]), spare
        for i in free:
            more = min(bound - given[i], max(1, budget * portions[i] // pool), spare)
            given[i] = given[i] + more
            spare = spare - more
    return np.array([bound] + given)


def ragged_sizes(stream_key, count, total, reach, skew):
    if count == 2:
        one = jax.random.randint(stream_key, (), max(1, total - reach), min(reach, total - 1) + 1)
        return jnp.stack([one, total - one])
    sizes = jnp.asarray(profile(count, total, reach, skew), jnp.int32)
    couples = (count - 1) // 2
    source_of, taker = sizes[1:1 + 2 * couples:2], sizes[2:2 + 2 * couples:2]
    margin = jnp.minimum(source_of - 1, reach - taker)
    moved = jax.random.randint(jax.random.fold_in(stream_key, 1), (couples,), 0, 1 << 20) % (margin + 1)
    sizes = sizes.at[1:1 + 2 * couples:2].set(source_of - moved).at[2:2 + 2 * couples:2].set(taker + moved)
    return sizes[jax.random.permutation(jax.random.fold_in(stream_key, 2), count)]


def bell_draw(rng, shape, width, reach, cuts=(), kind=jnp.bfloat16):
    level = block_levels(rng, shape, cuts, -0.22, 0.18) if cuts else 1.0
    values = jax.random.normal(rng, shape, jnp.float32) * width * level
    return jnp.minimum(jnp.maximum(values, -reach), reach).astype(kind)


def setup_inputs(seed: int = 0) -> dict:
    key_list = jax.random.split(jax.random.key(seed), 10)
    return {
        "seq_ids": jnp.searchsorted(jnp.cumsum(ragged_sizes(key_list[0], SEQS, TOKENS, MOST, 2)), jnp.arange(TOKENS), side="right").astype(jnp.int32),
        "query_inputs": bell_draw(key_list[1], (TOKENS, D), 1.0, 6.0, ((0, 32), (1, 16))),
        "query_grads": bell_draw(key_list[2], (TOKENS, D), MOST ** -0.5, 0.25, ((0, 16), (1, 32))),
        "query_act_basis": bell_draw(key_list[3], (D, D), D ** -0.5, 0.0625, ((0, 16), (1, 32))),
        "query_grad_basis": bell_draw(key_list[4], (D, D), D ** -0.5, 0.0625, ((0, 32), (1, 16))),
        "output_inputs": bell_draw(key_list[5], (TOKENS, D), 1.0, 6.0, ((0, 32), (1, 16))),
        "output_grads": bell_draw(key_list[6], (TOKENS, D), MOST ** -0.5, 0.25, ((0, 16), (1, 32))),
        "output_act_basis": bell_draw(key_list[7], (D, D), D ** -0.5, 0.0625, ((0, 16), (1, 32))),
        "output_grad_basis": bell_draw(key_list[8], (D, D), D ** -0.5, 0.0625, ((0, 32), (1, 16))),
    }


def rotate(tokens, eigen_basis):
    return jnp.dot(tokens, eigen_basis, preferred_element_type=jnp.float32)


def correct(act_rot, grad_rot, seq_ids):
    numbers = jnp.arange(SEQS, dtype=jnp.int32)
    counts = jnp.sum((seq_ids[None, :] == numbers[:, None]).astype(jnp.int32), axis=1).astype(jnp.int32)
    starts = (jnp.cumsum(counts) - counts).astype(jnp.int32)
    padded_act = jnp.concatenate([act_rot, jnp.zeros((MOST, act_rot.shape[1]), act_rot.dtype)], 0)
    padded_grad = jnp.concatenate([grad_rot, jnp.zeros((MOST, grad_rot.shape[1]), grad_rot.dtype)], 0)
    offsets = jnp.arange(MOST, dtype=jnp.int32)
    running = jnp.zeros((grad_rot.shape[1], act_rot.shape[1]), jnp.float32)
    for seq_index in range(SEQS):
        act_rows = lax.dynamic_slice_in_dim(padded_act, starts[seq_index], MOST, 0)
        grad_rows = lax.dynamic_slice_in_dim(padded_grad, starts[seq_index], MOST, 0)
        inside = offsets < counts[seq_index]
        grad_rows = jnp.where(inside[:, None], grad_rows, jnp.zeros_like(grad_rows))
        product = lax.dot_general(grad_rows, act_rows, (((0,), (0,)), ((), ())), precision=lax.Precision.HIGHEST)
        running = running + product * product
    return running / SEQS


def reference(seq_ids, query_inputs, query_grads, query_act_basis, query_grad_basis, output_inputs, output_grads, output_act_basis, output_grad_basis):
    query_corr = correct(rotate(query_inputs, query_act_basis), rotate(query_grads, query_grad_basis), seq_ids)
    output_corr = correct(rotate(output_inputs, output_act_basis), rotate(output_grads, output_grad_basis), seq_ids)
    return (query_corr, output_corr)
```

```python
import jax
import jax.numpy as jnp
from jax import lax
from jax.sharding import Mesh, PartitionSpec as P

SEQS = 4
ROW = ("xl", "y", "c")
Z = ("zh", "zl")
PLANE = ("xh", "xl", "y", "c")
NZ = 16
NEAR = (0, 1, -1, 2)
FAR = (0, 4, -4, 8)
TOP = 32000.0


def shift(x, by):
    if by == 0:
        return x
    return lax.ppermute(x, Z, [(i, (i + by) % NZ) for i in range(NZ)])


def swap_half(x):
    return lax.ppermute(x, "xh", [(0, 1), (1, 0)])


def pack(x):
    b, p, t, n = x.shape
    most = jnp.max(jnp.abs(x), axis=(2, 3), keepdims=True)
    step = jnp.ceil(jnp.log2(jnp.maximum(most, 1e-30)) * 64.0)
    codes = jnp.round(x * (TOP * jnp.exp2(step * (-1.0 / 64.0)))).astype(jnp.int16)
    head = jnp.broadcast_to(step.astype(jnp.int16), (b, p, 4, n))
    return jnp.concatenate([codes.reshape(b, p * t, n), head.reshape(b, 8, n)], axis=1)


def unpack(w):
    b, rows, n = w.shape
    t = (rows - 8) // 2
    step = jnp.stack([w[:, rows - 8, :1], w[:, rows - 4, :1]], axis=1).astype(jnp.float32)
    scale = jnp.exp2(step * (1.0 / 64.0)) * (1.0 / TOP)
    return w[:, : 2 * t].reshape(b, 2, t, n).astype(jnp.float32) * scale[..., None]


def roll_blocks(x, by):
    return lax.dynamic_slice_in_dim(jnp.concatenate([x, x], 0), by, x.shape[0], 0)


def reduce_scatter_z(part):
    def group(near):
        return jnp.stack([part[(near + far) % NZ] for far in FAR])

    total = group(0)
    for near in NEAR[1:]:
        total = total + unpack(shift(pack(group(near)), near))
    result = total[0]
    for index, far in enumerate(FAR[1:]):
        result = result + unpack(shift(pack(total[index + 1:index + 2]), far))[0]
    return result


def gather_z(w):
    level = jnp.concatenate([shift(w, far) for far in FAR], 0)
    both = jnp.concatenate([shift(level, near) for near in NEAR], 0)
    offsets = [(near + far) % NZ for near in NEAR for far in FAR]
    order = [offsets.index(i) for i in range(NZ)]
    return jnp.concatenate([both[k:k + 1] for k in order], 0)


def correct(act_rot, grad_rot, seq_ids):
    running = jnp.zeros((grad_rot.shape[1], act_rot.shape[1]), jnp.float32)
    for seq in range(SEQS):
        grad_rows = jnp.where((seq_ids == seq)[:, None], grad_rot, 0.0)
        product = lax.dot_general(
            grad_rows, act_rot, (((0,), (0,)), ((), ())), precision=lax.Precision.HIGH
        )
        running = running + product * product
    return running / SEQS


def dot(a, b):
    return jnp.dot(a, b, preferred_element_type=jnp.float32)


def per_device(seq_ids, qx, qg, qa, qb, ox, og, oa, ob):
    z = lax.axis_index(Z)
    xh = lax.axis_index("xh")
    mine_first = xh == 0

    grads = jnp.stack([qg, og])
    sent = jnp.transpose(grads.reshape(2, 2, 32, 256), (1, 0, 2, 3))
    sent = jnp.broadcast_to(sent[:, None], (2, 16, 2, 32, 256)).reshape(32, 2, 32, 256)
    got = lax.all_to_all(sent, PLANE, split_axis=0, concat_axis=0, tiled=True)
    grad_basis = jnp.stack([qb, ob])
    grad_other = swap_half(grad_basis)
    inputs = lax.all_gather(jnp.stack([qx, ox])[None], Z, axis=0, tiled=True)
    act_basis = jnp.stack([qa, oa])
    act_other = swap_half(act_basis)

    got = got.reshape(2, 16, 2, 32, 256)
    g0 = roll_blocks(got[0], z)
    g1 = roll_blocks(got[1], z)
    b0 = jnp.where(mine_first, grad_basis, grad_other)
    b1 = jnp.where(mine_first, grad_other, grad_basis)
    parts = []
    for p in range(2):
        part = dot(g0[:, p].reshape(512, 256), b0[p]) + dot(g1[:, p].reshape(512, 256), b1[p])
        parts.append(part.reshape(16, 32, 512))
    part = jnp.stack(parts, 1)
    grad_mine = reduce_scatter_z(part)
    words = gather_z(pack(grad_mine[None]))
    others = swap_half(words)

    a0 = jnp.where(mine_first, act_basis, act_other)
    a1 = jnp.where(mine_first, act_other, act_basis)
    parts = []
    for p in range(2):
        rows = inputs[:, p].reshape(512, 512)
        part = jnp.concatenate([dot(rows, a0[p]), dot(rows, a1[p])], 1)
        parts.append(part.reshape(16, 32, 512))
    act_words = pack(jnp.stack(parts, 1))
    act_words = lax.all_to_all(act_words, ROW, split_axis=0, concat_axis=0, tiled=True)
    act_mine = jnp.sum(unpack(act_words), axis=0)
    act_sent = pack(jnp.stack([act_mine[:, :, :256], act_mine[:, :, 256:]]))
    act_sent = jnp.broadcast_to(act_sent[:, None], (2, 16, 72, 256)).reshape(32, 72, 256)
    act_words = lax.all_to_all(act_sent, PLANE, split_axis=0, concat_axis=0, tiled=True)
    act = jnp.transpose(unpack(act_words), (1, 0, 2, 3)).reshape(2, 1024, 256)

    low = jnp.where(mine_first, words, others)
    high = jnp.where(mine_first, others, words)
    both = jnp.stack([low, high])
    both = lax.rev(both, (1,))
    both = lax.dynamic_slice_in_dim(jnp.concatenate([both, both], 1), NZ - 1 - z, NZ, 1)
    grad = unpack(both.reshape(32, 72, 512)).reshape(2, 16, 2, 32, 512)
    grad = jnp.transpose(grad, (2, 1, 0, 3, 4)).reshape(2, 1024, 512)
    return correct(act[0], grad[0], seq_ids), correct(act[1], grad[1], seq_ids)


def solution(mesh):
    fine = Mesh(mesh.devices.reshape(2, 4, 2, 2, 4, 4), ("xl", "y", "c", "xh", "zh", "zl"))
    row, col = ROW, ("xh",) + Z
    in_specs = (P(), P(col, row), P(row, col), P(row, col), P(col, row)) + (
        P(col, row),
        P(row, col),
        P(row, col),
        P(col, row),
    )
    out_specs = (P(row, col), P(row, col))
    return jax.shard_map(
        per_device, mesh=fine, in_specs=in_specs, out_specs=out_specs, check_vma=False
    )
```

```python
import jax
import jax.numpy as jnp
from jax import lax
from jax.experimental import pallas as pl
from jax.experimental.pallas import tpu as pltpu
from jax.sharding import Mesh, PartitionSpec as P

SEQS = 4
ROW = ("xl", "y", "c")
Z = ("zh", "zl")
PLANE = ("xh", "xl", "y", "c")
NZ = 16
NEAR = (0, 1, -1, 2)
TOP = 32000.0
F32 = jnp.float32
BF16 = jnp.bfloat16
S16 = jnp.int16


def shift(x, by):
    return lax.ppermute(x, Z, [(i, (i + by) % NZ) for i in range(NZ)])


def swap_half(x):
    return lax.ppermute(x, "xh", [(0, 1), (1, 0)])


def whole(kernel, outs, args, scratch=(), scalars=1, flops=0):
    specs = [
        pl.BlockSpec(memory_space=pltpu.SMEM if i < scalars else pltpu.VMEM)
        for i in range(len(args))
    ]
    moved = sum(a.size * a.dtype.itemsize for a in args) + sum(
        o.size * o.dtype.itemsize for o in outs
    )
    return pl.pallas_call(
        kernel,
        out_shape=outs,
        in_specs=specs,
        out_specs=[pl.BlockSpec(memory_space=pltpu.VMEM) for _ in outs],
        scratch_shapes=list(scratch),
        compiler_params=pltpu.CompilerParams(vmem_limit_bytes=40 * 2**20),
        cost_estimate=pl.CostEstimate(flops=flops, bytes_accessed=moved, transcendentals=0),
    )(*args)


def coded(x):
    most = jnp.max(jnp.max(jnp.abs(x), axis=1, keepdims=True), axis=0, keepdims=True)
    step = jnp.ceil(jnp.log2(jnp.maximum(most, 1e-30)) * 64.0)
    return jnp.round(x * (TOP * jnp.exp2(step * (-1.0 / 64.0)))), step


def message(x0, x1):
    (c0, s0), (c1, s1) = coded(x0), coded(x1)
    n = x0.shape[1]
    head = jnp.where(lax.broadcasted_iota(jnp.int32, (8, n), 0) < 4, s0, s1)
    return jnp.concatenate([c0, c1, head], axis=0).astype(jnp.int32).astype(S16)


def opened(w, t):
    x = w.astype(F32)
    scale = jnp.exp2(x[2 * t:] * (1.0 / 64.0)) * (1.0 / TOP)
    return x[:t] * scale[0:1], x[t:2 * t] * scale[4:5]


def rotate_grad_kernel(where, got, qb, ob, other, keep, *sends):
    z, xh = where[0], where[1]
    for index, near in enumerate(NEAR):
        residue = lax.rem(z + near + NZ, 4)
        done = []
        for p in range(2):
            basis = (qb, ob)[p]
            rows = [
                jnp.concatenate([got[side, 4 * j + residue, p] for j in range(4)], axis=0)
                for side in (xh, 1 - xh)
            ]
            done.append(
                jnp.dot(rows[0], basis[...], preferred_element_type=F32)
                + jnp.dot(rows[1], other[p], preferred_element_type=F32)
            )
        for j in range(4):
            parts = [d[32 * j:32 * j + 32] for d in done]
            if near == 0:
                keep[j, 0], keep[j, 1] = parts
            else:
                sends[index - 1][j] = message(*parts)


def near_sum_kernel(keep, w1, w2, w3, out):
    for j in range(4):
        total = [keep[j, 0], keep[j, 1]]
        for w in (w1, w2, w3):
            parts = opened(w[j], 32)
            total = [total[0] + parts[0], total[1] + parts[1]]
        out[j] = message(*total)


def far_sum_kernel(w, out):
    total = opened(w[0], 32)
    for j in range(1, 4):
        parts = opened(w[j], 32)
        total = [total[0] + parts[0], total[1] + parts[1]]
    out[0] = message(*total)


def rotate_act_kernel(x0, x1, x2, x3, qa, oa, other, out):
    for index, x in enumerate((x0, x1, x2, x3)):
        done = []
        for p in range(2):
            rows = jnp.concatenate([x[j, p] for j in range(4)], axis=0)
            basis = (qa, oa)[p]
            done.append(
                jnp.concatenate(
                    [
                        jnp.dot(rows, basis[...], preferred_element_type=F32),
                        jnp.dot(rows, other[p], preferred_element_type=F32),
                    ],
                    axis=1,
                )
            )
        for j in range(4):
            out[4 * index + j] = message(*[d[32 * j:32 * j + 32] for d in done])


def act_sum_kernel(where, w, out):
    xh = where[1]
    total = opened(w[0], 32)
    for e in range(1, 16):
        parts = opened(w[e], 32)
        total = [total[0] + parts[0], total[1] + parts[1]]
    out[xh] = message(total[0][:, :256], total[1][:, :256])
    out[1 - xh] = message(total[0][:, 256:], total[1][:, 256:])


def correct_kernel(where, act_w, *rest):
    grads, (q_out, o_out, act, high, low, acc) = rest[:8], rest[8:]
    z, xh = where[0], where[1]
    for p in range(2):
        out = (q_out, o_out)[p]

        def place_act(e, carry, p=p):
            side, r = e // 16, lax.rem(e, 16)
            near = jnp.where(r // 4 == 2, -1, jnp.where(r // 4 == 3, 2, r // 4))
            block = 4 * lax.rem(r, 4) + lax.rem(z - near + NZ, 4)
            at = pl.multiple_of(512 * side + 32 * block, 32)
            act[pl.ds(at, 32), :] = opened(act_w[e], 32)[p]
            return carry

        lax.fori_loop(0, 32, place_act, 0)
        for side in range(2):
            half = xh if side == 0 else 1 - xh
            for index, near in enumerate(NEAR):
                words = grads[4 * side + index]

                def place_grad(j, carry, p=p, near=near, half=half, words=words):
                    block = 4 * j + lax.rem(z - near + NZ, 4)
                    at = pl.multiple_of(64 * block + 32 * half, 32)
                    x = opened(words[j], 32)[p]
                    top = x.astype(BF16)
                    high[pl.ds(at, 32), :] = top
                    low[pl.ds(at, 32), :] = (x - top.astype(F32)).astype(BF16)
                    return carry

                lax.fori_loop(0, 4, place_grad, 0)
        for seq in range(SEQS):
            first, last = where[2 + seq], where[3 + seq]
            acc[...] = jnp.zeros_like(acc)

            def chunk(k, carry, first=first, last=last):
                at = pl.multiple_of(256 * k, 256)
                token = at + lax.broadcasted_iota(jnp.int32, (256, 256), 0)
                a = jnp.where((token >= first) & (token < last), act[pl.ds(at, 256), :], 0.0)
                a_high = a.astype(BF16)
                a_low = (a - a_high.astype(F32)).astype(BF16)
                g_high, g_low = high[pl.ds(at, 256), :], low[pl.ds(at, 256), :]
                dims = (((0,), (0,)), ((), ()))
                acc[...] += (
                    lax.dot_general(g_high, a_high, dims, preferred_element_type=F32)
                    + lax.dot_general(g_high, a_low, dims, preferred_element_type=F32)
                    + lax.dot_general(g_low, a_high, dims, preferred_element_type=F32)
                )
                return carry

            lax.fori_loop(first // 256, (last + 255) // 256, chunk, 0)
            square = acc[...] * acc[...]
            if seq == 0:
                out[...] = square
            elif seq < SEQS - 1:
                out[...] += square
            else:
                out[...] = (out[...] + square) * (1.0 / SEQS)


def shape(*dims, dtype=S16):
    return jax.ShapeDtypeStruct(dims, dtype)


def per_device(seq_ids, qx, qg, qa, qb, ox, og, oa, ob):
    z = lax.axis_index(Z)
    xh = lax.axis_index("xh")
    bounds = jnp.sum(
        (seq_ids[None, :] < jnp.arange(SEQS + 1, dtype=jnp.int32)[:, None]).astype(jnp.int32), axis=1
    )
    where = jnp.concatenate([jnp.stack([z, xh]).astype(jnp.int32), bounds, jnp.zeros(1, jnp.int32)])

    grads = jnp.stack([qg, og])
    sent = jnp.transpose(grads.reshape(2, 2, 32, 256), (1, 0, 2, 3))
    sent = jnp.broadcast_to(sent[:, None], (2, 16, 2, 32, 256)).reshape(32, 2, 32, 256)
    got = lax.all_to_all(sent, PLANE, split_axis=0, concat_axis=0, tiled=True)
    got = got.reshape(2, 16, 2, 32, 256)
    grad_other = swap_half(jnp.stack([qb, ob]))
    level = lax.all_gather(jnp.stack([qx, ox])[None], "zh", axis=0, tiled=True)
    inputs = [level] + [shift(level, near) for near in NEAR[1:]]
    act_other = swap_half(jnp.stack([qa, oa]))

    keep, *sends = whole(
        rotate_grad_kernel,
        [shape(4, 2, 32, 512, dtype=F32)] + [shape(4, 72, 512)] * 3,
        [where, got, qb, ob, grad_other],
        flops=2 * 2 * 512 * 512 * 512,
    )
    sends = [shift(w, near) for w, near in zip(sends, NEAR[1:])]
    [words] = whole(near_sum_kernel, [shape(4, 72, 512)], [keep] + sends, scalars=0)
    words = lax.all_to_all(words, "zh", split_axis=0, concat_axis=0, tiled=True)
    [words] = whole(far_sum_kernel, [shape(1, 72, 512)], [words], scalars=0)
    words = lax.all_gather(words, "zh", axis=0, tiled=True)
    mine = [words] + [shift(words, near) for near in NEAR[1:]]
    others = [swap_half(w) for w in mine]

    [act_words] = whole(
        rotate_act_kernel,
        [shape(16, 72, 512)],
        inputs + [qa, oa, act_other],
        scalars=0,
        flops=2 * 2 * 512 * 512 * 512,
    )
    act_words = lax.all_to_all(act_words, ROW, split_axis=0, concat_axis=0, tiled=True)
    [act_words] = whole(act_sum_kernel, [shape(2, 72, 256)], [where, act_words])
    act_words = jnp.broadcast_to(act_words[:, None], (2, 16, 72, 256)).reshape(32, 72, 256)
    act_words = lax.all_to_all(act_words, PLANE, split_axis=0, concat_axis=0, tiled=True)

    return tuple(
        whole(
            correct_kernel,
            [shape(512, 256, dtype=F32)] * 2,
            [where, act_words] + mine + others,
            scratch=[
                pltpu.VMEM((1024, 256), F32),
                pltpu.VMEM((1024, 512), BF16),
                pltpu.VMEM((1024, 512), BF16),
                pltpu.VMEM((512, 256), F32),
            ],
            flops=2 * 2 * 7 * 3 * 256 * 512 * 256,
        )
    )


def solution(mesh):
    fine = Mesh(mesh.devices.reshape(2, 4, 2, 2, 4, 4), ("xl", "y", "c", "xh", "zh", "zl"))
    row, col = ROW, ("xh",) + Z
    one = (P(col, row), P(row, col), P(row, col), P(col, row))
    out_specs = (P(row, col), P(row, col))
    return jax.shard_map(
        per_device, mesh=fine, in_specs=(P(),) + one + one, out_specs=out_specs, check_vma=False
    )
```

```python
import jax
import jax.numpy as jnp
from jax import lax
from jax.experimental import pallas as pl
from jax.experimental.pallas import tpu as pltpu
from jax.sharding import Mesh, PartitionSpec as P

SEQS = 4
ROW = ("xl", "y", "c")
Z = ("zh", "zm", "zl")
Z8 = ("zh", "zm")
ZH = "zh"
PLANE = ("xh", "xl", "y", "c")
NZ = 16
TOP = 32000.0
F32 = jnp.float32
BF16 = jnp.bfloat16
S16 = jnp.int16


def shift(x, by):
    return lax.ppermute(x, Z, [(i, (i + by) % NZ) for i in range(NZ)])


def swap_half(x):
    return lax.ppermute(x, "xh", [(0, 1), (1, 0)])


def whole(kernel, outs, args, scratch=(), scalars=1, flops=0):
    specs = [
        pl.BlockSpec(memory_space=pltpu.SMEM if i < scalars else pltpu.VMEM)
        for i in range(len(args))
    ]
    moved = sum(a.size * a.dtype.itemsize for a in args) + sum(
        o.size * o.dtype.itemsize for o in outs
    )
    return pl.pallas_call(
        kernel,
        out_shape=outs,
        in_specs=specs,
        out_specs=[pl.BlockSpec(memory_space=pltpu.VMEM) for _ in outs],
        scratch_shapes=list(scratch),
        compiler_params=pltpu.CompilerParams(vmem_limit_bytes=40 * 2**20),
        cost_estimate=pl.CostEstimate(flops=flops, bytes_accessed=moved, transcendentals=0),
    )(*args)


def coded(x):
    most = jnp.max(jnp.max(jnp.abs(x), axis=1, keepdims=True), axis=0, keepdims=True)
    step = jnp.ceil(jnp.log2(jnp.maximum(most, 1e-30)) * 64.0)
    return jnp.round(x * (TOP * jnp.exp2(step * (-1.0 / 64.0)))), step


def message(*blocks):
    pieces = [coded(x) for x in blocks]
    head = pieces[0][1]
    if len(blocks) == 2:
        row = lax.broadcasted_iota(jnp.int32, (8, blocks[0].shape[1]), 0)
        head = jnp.where(row < 4, head, pieces[1][1])
    head = jnp.broadcast_to(head, (8, blocks[0].shape[1]))
    return jnp.concatenate([c for c, _ in pieces] + [head], axis=0).astype(jnp.int32).astype(S16)


def opened(w, t):
    x = w.astype(F32)
    blocks = x.shape[0] // t
    scale = jnp.exp2(x[blocks * t:] * (1.0 / 64.0)) * (1.0 / TOP)
    return [x[t * i:t * i + t] * scale[4 * i:4 * i + 1] for i in range(blocks)]


def added(*pairs):
    return [sum(terms[1:], terms[0]) for terms in zip(*pairs)]


def rotate_grad_kernel(where, got, qb, ob, other, keep, near1, near3, two_up, two_down):
    z, xh = where[0], where[1]
    for ahead in (1, 3, 2, 0):
        residue = lax.rem(z + ahead, 4)
        done = []
        for p in range(2):
            basis = (qb, ob)[p]
            rows = [
                jnp.concatenate([got[side, 4 * j + residue, p] for j in range(4)], axis=0)
                for side in (xh, 1 - xh)
            ]
            done.append(
                jnp.dot(rows[0], basis[...], preferred_element_type=F32)
                + jnp.dot(rows[1], other[p], preferred_element_type=F32)
            )
        for j in range(4):
            parts = [d[32 * j:32 * j + 32] for d in done]
            if ahead == 0:
                keep[j, 0], keep[j, 1] = parts
            elif ahead == 2:
                (two_up, two_down)[j // 2][j % 2] = message(*parts)
            else:
                (near1 if ahead == 1 else near3)[j] = message(*parts)


def near_sum_kernel(keep, w1, w3, up, down, out):
    for j in range(4):
        two = up if j < 2 else down
        out[j] = message(
            *added(
                [keep[j, 0], keep[j, 1]],
                opened(w1[j], 32),
                opened(w3[j], 32),
                opened(two[j % 2], 32),
            )
        )


def far_sum_kernel(w, out):
    out[0] = message(*added(*[opened(w[j], 32) for j in range(4)]))


def rotate_act_kernel(where, level, x1, x3, up, down, qa, oa, other, out):
    for behind, x in ((0, level), (1, x1), (3, x3), (2, None)):
        done = []
        for p in range(2):
            basis = (qa, oa)[p]
            if x is None:
                rows = [up[0, p], up[1, p], down[0, p], down[1, p]]
            else:
                rows = [x[j, p] for j in range(4)]
            rows = jnp.concatenate(rows, axis=0)
            done.append(
                jnp.concatenate(
                    [
                        jnp.dot(rows, basis[...], preferred_element_type=F32),
                        jnp.dot(rows, other[p], preferred_element_type=F32),
                    ],
                    axis=1,
                )
            )
        residue = lax.rem(where[0] + 4 - behind, 4)
        for j in range(4):
            out[4 * j + residue] = message(*[d[32 * j:32 * j + 32] for d in done])


def act_sum_kernel(where, w, out):
    xh = where[1]
    total = opened(w[0], 32)
    for e in range(1, 16):
        total = added(total, opened(w[e], 32))
    mine = message(total[0][:, :256], total[1][:, :256])
    other = message(total[0][:, 256:], total[1][:, 256:])
    for r in range(16):
        out[xh, r] = mine
        out[1 - xh, r] = other


def open_act_kernel(w, out):
    for e in range(0, 32, 4):
        blocks = [opened(w[e + i], 32) for i in range(4)]
        for p in range(2):
            out[p, :, 32 * e:32 * e + 128] = jnp.concatenate([b[p] for b in blocks], axis=0).T


def correct_kernel(where, act, *rest):
    grads, (q_out, o_out, high, low, acc, total) = rest[:6], rest[6:]
    zl, xh = lax.rem(where[0], 2), where[1]
    for p in range(2):
        for side in range(2):
            half = xh if side == 0 else 1 - xh
            level, first_w, last_w = grads[3 * side:3 * side + 3]
            for k in range(16):
                w = level[k] if k < 8 else (first_w[k - 8] if k < 12 else last_w[k - 12])
                block = 2 * (k % 8) + (zl if k < 8 else 1 - zl)
                at = pl.multiple_of(64 * block + 32 * half, 32)
                x = opened(w, 32)[p]
                top = x.astype(BF16)
                high[pl.ds(at, 32), :] = top
                low[pl.ds(at, 32), :] = (x - top.astype(F32)).astype(BF16)
        for seq in range(SEQS):
            first, last = where[2 + seq], where[3 + seq]
            acc[...] = jnp.zeros_like(acc)

            def chunk(k, carry, first=first, last=last, p=p):
                at = pl.multiple_of(256 * k, 256)
                token = at + lax.broadcasted_iota(jnp.int32, (256, 256), 1)
                a = jnp.where((token >= first) & (token < last), act[p, :, pl.ds(at, 256)], 0.0)
                a_high = a.astype(BF16)
                a_low = (a - a_high.astype(F32)).astype(BF16)
                g_high, g_low = high[pl.ds(at, 256), :], low[pl.ds(at, 256), :]
                acc[...] += (
                    jnp.dot(a_high, g_high, preferred_element_type=F32)
                    + jnp.dot(a_low, g_high, preferred_element_type=F32)
                    + jnp.dot(a_high, g_low, preferred_element_type=F32)
                )
                return carry

            lax.fori_loop(first // 256, (last + 255) // 256, chunk, 0)
            square = acc[...] * acc[...]
            total[...] = square if seq == 0 else total[...] + square
        out = (q_out, o_out)[p]
        out[...] = total[...].T * (1.0 / SEQS)


def shape(*dims, dtype=S16):
    return jax.ShapeDtypeStruct(dims, dtype)


def per_device(seq_ids, qx, qg, qa, qb, ox, og, oa, ob):
    z = lax.axis_index(Z)
    xh = lax.axis_index("xh")
    bounds = jnp.sum(
        (seq_ids[None, :] < jnp.arange(SEQS + 1, dtype=jnp.int32)[:, None]).astype(jnp.int32), axis=1
    )
    where = jnp.concatenate([jnp.stack([z, xh]).astype(jnp.int32), bounds, jnp.zeros(1, jnp.int32)])

    grads = jnp.stack([qg, og])
    sent = jnp.transpose(grads.reshape(2, 2, 32, 256), (1, 0, 2, 3))
    sent = jnp.broadcast_to(sent[:, None], (2, 16, 2, 32, 256)).reshape(32, 2, 32, 256)
    got = lax.all_to_all(sent, PLANE, split_axis=0, concat_axis=0, tiled=True)
    got = got.reshape(2, 16, 2, 32, 256)
    grad_other = swap_half(jnp.stack([qb, ob]))
    level = lax.all_gather(jnp.stack([qx, ox])[None], ZH, axis=0, tiled=True)

    keep, *sends = whole(
        rotate_grad_kernel,
        [shape(4, 2, 32, 512, dtype=F32)] + [shape(4, 72, 512)] * 2 + [shape(2, 72, 512)] * 2,
        [where, got, qb, ob, grad_other],
        flops=2 * 2 * 512 * 512 * 512,
    )
    *sends, qa, oa, level = lax.optimization_barrier((*sends, qa, oa, level))
    sends = [shift(w, by) for w, by in zip(sends, (1, -1, 2, -2))]
    act_other = swap_half(jnp.stack([qa, oa]))
    [words] = whole(near_sum_kernel, [shape(4, 72, 512)], [keep] + sends, scalars=0)
    words, level = lax.optimization_barrier((words, level))
    inputs = [level] + [
        shift(w, by) for w, by in ((level, 1), (level, -1), (level[:2], 2), (level[2:], -2))
    ]
    words = lax.all_to_all(words, ZH, split_axis=0, concat_axis=0, tiled=True)
    [words] = whole(far_sum_kernel, [shape(1, 72, 512)], [words], scalars=0)

    [act_words] = whole(
        rotate_act_kernel,
        [shape(16, 72, 512)],
        [where] + inputs + [qa, oa, act_other],
        flops=2 * 2 * 512 * 512 * 512,
    )
    words, act_words = lax.optimization_barrier((words, act_words))
    act_words = lax.all_to_all(act_words, ROW, split_axis=0, concat_axis=0, tiled=True)

    words = lax.all_gather(words, Z8, axis=0, tiled=True)
    other = swap_half(words)
    words, act_words = lax.optimization_barrier((words, act_words))
    mine = [words, shift(words[:4], 1), shift(words[4:], -1)]
    others = [other, shift(other[:4], 1), shift(other[4:], -1)]

    [act_words] = whole(act_sum_kernel, [shape(2, 16, 72, 256)], [where, act_words])
    act_words = act_words.reshape(32, 72, 256)
    act_words = lax.all_to_all(act_words, PLANE, split_axis=0, concat_axis=0, tiled=True)
    [act] = whole(open_act_kernel, [shape(2, 256, 1024, dtype=F32)], [act_words], scalars=0)

    return tuple(
        whole(
            correct_kernel,
            [shape(512, 256, dtype=F32)] * 2,
            [where, act] + mine + others,
            scratch=[
                pltpu.VMEM((1024, 512), BF16),
                pltpu.VMEM((1024, 512), BF16),
                pltpu.VMEM((256, 512), F32),
                pltpu.VMEM((256, 512), F32),
            ],
            flops=2 * 2 * 7 * 3 * 256 * 512 * 256,
        )
    )


def solution(mesh):
    fine = Mesh(mesh.devices.reshape(2, 4, 2, 2, 4, 2, 2), ("xl", "y", "c", "xh") + Z)
    row, col = ROW, ("xh",) + Z
    one = (P(col, row), P(row, col), P(row, col), P(col, row))
    out_specs = (P(row, col), P(row, col))
    return jax.shard_map(
        per_device, mesh=fine, in_specs=(P(),) + one + one, out_specs=out_specs, check_vma=False
    )
```

```python
import jax
import jax.numpy as jnp
from jax import lax
from jax.experimental import pallas as pl
from jax.experimental.pallas import tpu as pltpu
from jax.sharding import Mesh, PartitionSpec as P

SEQS = 4
ROW = ("xl", "y", "c")
Z = ("zh", "zm", "zl")
Z8 = ("zh", "zm")
ZH = "zh"
PLANE = ("xh", "xl", "y", "c")
NZ = 16
TOP = 32000.0
F32 = jnp.float32
BF16 = jnp.bfloat16
S16 = jnp.int16


def shift(x, by):
    return lax.ppermute(x, Z, [(i, (i + by) % NZ) for i in range(NZ)])


def swap_half(x):
    return lax.ppermute(x, "xh", [(0, 1), (1, 0)])


def whole(kernel, outs, args, scratch=(), scalars=1, flops=0):
    specs = [
        pl.BlockSpec(memory_space=pltpu.SMEM if i < scalars else pltpu.VMEM)
        for i in range(len(args))
    ]
    moved = sum(a.size * a.dtype.itemsize for a in args) + sum(
        o.size * o.dtype.itemsize for o in outs
    )
    return pl.pallas_call(
        kernel,
        out_shape=outs,
        in_specs=specs,
        out_specs=[pl.BlockSpec(memory_space=pltpu.VMEM) for _ in outs],
        scratch_shapes=list(scratch),
        compiler_params=pltpu.CompilerParams(vmem_limit_bytes=40 * 2**20),
        cost_estimate=pl.CostEstimate(flops=flops, bytes_accessed=moved, transcendentals=0),
    )(*args)


def coded(x):
    most = jnp.max(jnp.max(jnp.abs(x), axis=1, keepdims=True), axis=0, keepdims=True)
    step = jnp.ceil(jnp.log2(jnp.maximum(most, 1e-30)) * 64.0)
    return jnp.round(x * (TOP * jnp.exp2(step * (-1.0 / 64.0)))), step


def message(*blocks):
    pieces = [coded(x) for x in blocks]
    head = pieces[0][1]
    if len(blocks) == 2:
        row = lax.broadcasted_iota(jnp.int32, (8, blocks[0].shape[1]), 0)
        head = jnp.where(row < 4, head, pieces[1][1])
    head = jnp.broadcast_to(head, (8, blocks[0].shape[1]))
    return jnp.concatenate([c for c, _ in pieces] + [head], axis=0).astype(jnp.int32).astype(S16)


def opened(w, t):
    x = w.astype(F32)
    blocks = x.shape[0] // t
    scale = jnp.exp2(x[blocks * t:] * (1.0 / 64.0)) * (1.0 / TOP)
    return [x[t * i:t * i + t] * scale[4 * i:4 * i + 1] for i in range(blocks)]


def added(*pairs):
    return [sum(terms[1:], terms[0]) for terms in zip(*pairs)]


def rotate_grad_kernel(where, got, qb, ob, other, keep, near1, near3, two_up, two_down):
    z, xh = where[0], where[1]
    mine = jnp.where(xh == 0, qb[...], ob[...])
    for ahead in (1, 3, 2, 0):
        residue = lax.rem(z + ahead, 4)
        rows = [
            jnp.concatenate([got[side, 4 * j + residue] for j in range(4)], axis=0)
            for side in (xh, 1 - xh)
        ]
        done = jnp.dot(rows[0], mine, preferred_element_type=F32) + jnp.dot(
            rows[1], other[...], preferred_element_type=F32
        )
        for j in range(4):
            part = done[64 * j:64 * j + 64]
            if ahead == 0:
                keep[j] = part
            elif ahead == 2:
                (two_up, two_down)[j // 2][j % 2] = message(part)
            else:
                (near1 if ahead == 1 else near3)[j] = message(part)


def near_sum_kernel(keep, w1, w3, up, down, out):
    for j in range(4):
        two = up if j < 2 else down
        total = opened(w1[j], 64)[0] + opened(w3[j], 64)[0] + opened(two[j % 2], 64)[0]
        out[j] = message(keep[j] + total)


def far_sum_kernel(w, out):
    total = opened(w[0], 64)[0]
    for j in range(1, 4):
        total = total + opened(w[j], 64)[0]
    out[0] = message(total)


def rotate_act_kernel(where, level, x1, x3, up, down, qa, oa, other, out):
    for behind, x in ((0, level), (1, x1), (3, x3), (2, None)):
        done = []
        for p in range(2):
            basis = (qa, oa)[p]
            if x is None:
                rows = [up[0, p], up[1, p], down[0, p], down[1, p]]
            else:
                rows = [x[j, p] for j in range(4)]
            rows = jnp.concatenate(rows, axis=0)
            done.append(
                jnp.concatenate(
                    [
                        jnp.dot(rows, basis[...], preferred_element_type=F32),
                        jnp.dot(rows, other[p], preferred_element_type=F32),
                    ],
                    axis=1,
                )
            )
        residue = lax.rem(where[0] + 4 - behind, 4)
        for j in range(4):
            out[4 * j + residue] = message(*[d[32 * j:32 * j + 32] for d in done])


def act_sum_kernel(where, w, out):
    xh = where[1]
    total = opened(w[0], 32)
    for e in range(1, 16):
        total = added(total, opened(w[e], 32))
    mine = message(total[0][:, :256], total[1][:, :256])
    other = message(total[0][:, 256:], total[1][:, 256:])
    for r in range(16):
        out[xh, r] = mine
        out[1 - xh, r] = other


def open_act_kernel(w, high, low):
    for e in range(0, 32, 4):
        blocks = [opened(w[e + i], 32) for i in range(4)]
        for p in range(2):
            x = jnp.concatenate([b[p] for b in blocks], axis=0).T
            top = x.astype(BF16)
            high[p, :, 32 * e:32 * e + 128] = top
            low[p, :, 32 * e:32 * e + 128] = (x - top.astype(F32)).astype(BF16)


def correct_kernel(where, act_high, act_low, *rest):
    grads, (q_out, o_out, high, low, acc, total) = rest[:6], rest[6:]
    zl, xh = lax.rem(where[0], 2), where[1]
    for side in range(2):
        half = xh if side == 0 else 1 - xh
        level, first_w, last_w = grads[3 * side:3 * side + 3]
        for k in range(16):
            w = level[k] if k < 8 else (first_w[k - 8] if k < 12 else last_w[k - 12])
            block = 2 * (k % 8) + (zl if k < 8 else 1 - zl)
            at = pl.multiple_of(64 * block, 64)
            [x] = opened(w, 64)
            top = x.astype(BF16)
            high[half, pl.ds(at, 64), :] = top
            low[half, pl.ds(at, 64), :] = (x - top.astype(F32)).astype(BF16)
    for seq in range(SEQS):
        first, last = where[2 + seq], where[3 + seq]
        acc[...] = jnp.zeros_like(acc)

        def chunk(k, carry, first=first, last=last):
            at = pl.multiple_of(256 * k, 256)
            token = at + lax.broadcasted_iota(jnp.int32, (1, 256), 1)
            inside = ((token >= first) & (token < last)).astype(F32).astype(BF16)
            for p in range(2):
                a_high = act_high[p, :, pl.ds(at, 256)] * inside
                a_low = act_low[p, :, pl.ds(at, 256)] * inside
                g_high, g_low = high[p, pl.ds(at, 256), :], low[p, pl.ds(at, 256), :]
                acc[p] += (
                    jnp.dot(a_high, g_high, preferred_element_type=F32)
                    + jnp.dot(a_low, g_high, preferred_element_type=F32)
                    + jnp.dot(a_high, g_low, preferred_element_type=F32)
                )
            return carry

        lax.fori_loop(first // 256, (last + 255) // 256, chunk, 0)
        square = acc[...] * acc[...]
        total[...] = square if seq == 0 else total[...] + square
    q_out[...] = total[0].T * (1.0 / SEQS)
    o_out[...] = total[1].T * (1.0 / SEQS)


def shape(*dims, dtype=S16):
    return jax.ShapeDtypeStruct(dims, dtype)


def per_device(seq_ids, qx, qg, qa, qb, ox, og, oa, ob):
    z = lax.axis_index(Z)
    xh = lax.axis_index("xh")
    bounds = jnp.sum(
        (seq_ids[None, :] < jnp.arange(SEQS + 1, dtype=jnp.int32)[:, None]).astype(jnp.int32), axis=1
    )
    where = jnp.concatenate([jnp.stack([z, xh]).astype(jnp.int32), bounds, jnp.zeros(1, jnp.int32)])

    grads = jnp.stack([qg, og])
    sent = jnp.broadcast_to(grads[:, None], (2, 16, 64, 256)).reshape(32, 64, 256)
    got = lax.all_to_all(sent, PLANE, split_axis=0, concat_axis=0, tiled=True)
    got = got.reshape(2, 16, 64, 256)
    grad_other = swap_half(jnp.where(xh == 0, ob, qb))
    level = lax.all_gather(jnp.stack([qx, ox])[None], ZH, axis=0, tiled=True)

    keep, *sends = whole(
        rotate_grad_kernel,
        [shape(4, 64, 512, dtype=F32)] + [shape(4, 72, 512)] * 2 + [shape(2, 72, 512)] * 2,
        [where, got, qb, ob, grad_other],
        flops=2 * 2 * 512 * 512 * 512,
    )
    *sends, qa, oa, level = lax.optimization_barrier((*sends, qa, oa, level))
    sends = [shift(w, by) for w, by in zip(sends, (1, -1, 2, -2))]
    act_other = swap_half(jnp.stack([qa, oa]))
    [words] = whole(near_sum_kernel, [shape(4, 72, 512)], [keep] + sends, scalars=0)
    words, level = lax.optimization_barrier((words, level))
    inputs = [level] + [
        shift(w, by) for w, by in ((level, 1), (level, -1), (level[:2], 2), (level[2:], -2))
    ]
    words = lax.all_to_all(words, ZH, split_axis=0, concat_axis=0, tiled=True)
    [words] = whole(far_sum_kernel, [shape(1, 72, 512)], [words], scalars=0)

    [act_words] = whole(
        rotate_act_kernel,
        [shape(16, 72, 512)],
        [where] + inputs + [qa, oa, act_other],
        flops=2 * 2 * 512 * 512 * 512,
    )
    words, act_words = lax.optimization_barrier((words, act_words))
    act_words = lax.all_to_all(act_words, ROW, split_axis=0, concat_axis=0, tiled=True)

    words = lax.all_gather(words, Z8, axis=0, tiled=True)
    other = swap_half(words)
    words, act_words = lax.optimization_barrier((words, act_words))
    mine = [words, shift(words[:4], 1), shift(words[4:], -1)]
    others = [other, shift(other[:4], 1), shift(other[4:], -1)]

    [act_words] = whole(act_sum_kernel, [shape(2, 16, 72, 256)], [where, act_words])
    act_words = act_words.reshape(32, 72, 256)
    act_words = lax.all_to_all(act_words, PLANE, split_axis=0, concat_axis=0, tiled=True)
    act = whole(open_act_kernel, [shape(2, 256, 1024, dtype=BF16)] * 2, [act_words], scalars=0)

    return tuple(
        whole(
            correct_kernel,
            [shape(512, 256, dtype=F32)] * 2,
            [where] + list(act) + mine + others,
            scratch=[
                pltpu.VMEM((2, 1024, 512), BF16),
                pltpu.VMEM((2, 1024, 512), BF16),
                pltpu.VMEM((2, 256, 512), F32),
                pltpu.VMEM((2, 256, 512), F32),
            ],
            flops=2 * 2 * 7 * 3 * 256 * 512 * 256,
        )
    )


def solution(mesh):
    fine = Mesh(mesh.devices.reshape(2, 4, 2, 2, 4, 2, 2), ("xl", "y", "c", "xh") + Z)
    row, col = ROW, ("xh",) + Z
    one = (P(col, row), P(row, col), P(row, col), P(col, row))
    out_specs = (P(row, col), P(row, col))
    return jax.shard_map(
        per_device, mesh=fine, in_specs=(P(),) + one + one, out_specs=out_specs, check_vma=False
    )
```

```python
import jax
import jax.numpy as jnp
from jax import lax
from jax.experimental import pallas as pl
from jax.experimental.pallas import tpu as pltpu
from jax.sharding import Mesh, PartitionSpec as P

SEQS = 4
ROW = ("xl", "y", "c")
Z = ("zh", "zm", "zl")
Z8 = ("zh", "zm")
ZH = "zh"
PLANE = ("xh", "xl", "y", "c")
NZ = 16
TOP = 32000.0
F32 = jnp.float32
BF16 = jnp.bfloat16
S16 = jnp.int16


def shift(x, by):
    return lax.ppermute(x, Z, [(i, (i + by) % NZ) for i in range(NZ)])


def swap_half(x):
    return lax.ppermute(x, "xh", [(0, 1), (1, 0)])


def whole(kernel, outs, args, scratch=(), scalars=1, flops=0):
    specs = [
        pl.BlockSpec(memory_space=pltpu.SMEM if i < scalars else pltpu.VMEM)
        for i in range(len(args))
    ]
    moved = sum(a.size * a.dtype.itemsize for a in args) + sum(
        o.size * o.dtype.itemsize for o in outs
    )
    return pl.pallas_call(
        kernel,
        out_shape=outs,
        in_specs=specs,
        out_specs=[pl.BlockSpec(memory_space=pltpu.VMEM) for _ in outs],
        scratch_shapes=list(scratch),
        compiler_params=pltpu.CompilerParams(vmem_limit_bytes=40 * 2**20),
        cost_estimate=pl.CostEstimate(flops=flops, bytes_accessed=moved, transcendentals=0),
    )(*args)


def coded(x):
    most = jnp.max(jnp.max(jnp.abs(x), axis=1, keepdims=True), axis=0, keepdims=True)
    step = jnp.ceil(jnp.log2(jnp.maximum(most, 1e-30)) * 64.0)
    return jnp.round(x * (TOP * jnp.exp2(step * (-1.0 / 64.0)))), step


def message(*blocks):
    pieces = [coded(x) for x in blocks]
    head = pieces[0][1]
    if len(blocks) == 2:
        row = lax.broadcasted_iota(jnp.int32, (8, blocks[0].shape[1]), 0)
        head = jnp.where(row < 4, head, pieces[1][1])
    head = jnp.broadcast_to(head, (8, blocks[0].shape[1]))
    return jnp.concatenate([c for c, _ in pieces] + [head], axis=0).astype(jnp.int32).astype(S16)


def opened(w, t):
    x = w.astype(F32)
    blocks = x.shape[0] // t
    scale = jnp.exp2(x[blocks * t:] * (1.0 / 64.0)) * (1.0 / TOP)
    return [x[t * i:t * i + t] * scale[4 * i:4 * i + 1] for i in range(blocks)]


def added(*pairs):
    return [sum(terms[1:], terms[0]) for terms in zip(*pairs)]


def rotate_grad_kernel(where, got, qb, ob, other, keep, near1, near3, two_up, two_down):
    z, xh = where[0], where[1]
    mine = jnp.where(xh == 0, qb[...], ob[...])
    for ahead in (1, 3, 2, 0):
        residue = lax.rem(z + ahead, 4)
        rows = [
            jnp.concatenate([got[side, 4 * j + residue] for j in range(4)], axis=0)
            for side in (xh, 1 - xh)
        ]
        done = jnp.dot(rows[0], mine, preferred_element_type=F32) + jnp.dot(
            rows[1], other[...], preferred_element_type=F32
        )
        for j in range(4):
            part = done[64 * j:64 * j + 64]
            if ahead == 0:
                keep[j] = part
            elif ahead == 2:
                (two_up, two_down)[j // 2][j % 2] = message(part)
            else:
                (near1 if ahead == 1 else near3)[j] = message(part)


def near_sum_kernel(keep, w1, w3, up, down, out):
    for j in range(4):
        two = up if j < 2 else down
        total = opened(w1[j], 64)[0] + opened(w3[j], 64)[0] + opened(two[j % 2], 64)[0]
        out[j] = message(keep[j] + total)


def far_sum_kernel(w, out):
    total = opened(w[0], 64)[0]
    for j in range(1, 4):
        total = total + opened(w[j], 64)[0]
    out[0] = message(total)


def rotate_act_kernel(where, level, x1, x3, up, down, qa, oa, other, out):
    for behind, x in ((0, level), (1, x1), (3, x3), (2, None)):
        done = []
        for p in range(2):
            basis = (qa, oa)[p]
            if x is None:
                rows = [up[0, p], up[1, p], down[0, p], down[1, p]]
            else:
                rows = [x[j, p] for j in range(4)]
            rows = jnp.concatenate(rows, axis=0)
            done.append(
                jnp.concatenate(
                    [
                        jnp.dot(rows, basis[...], preferred_element_type=F32),
                        jnp.dot(rows, other[p], preferred_element_type=F32),
                    ],
                    axis=1,
                )
            )
        residue = lax.rem(where[0] + 4 - behind, 4)
        for j in range(4):
            out[4 * j + residue] = message(*[d[32 * j:32 * j + 32] for d in done])


def act_sum_kernel(where, w, out):
    xh = where[1]
    total = opened(w[0], 32)
    for e in range(1, 16):
        total = added(total, opened(w[e], 32))
    mine = message(total[0][:, :256], total[1][:, :256])
    other = message(total[0][:, 256:], total[1][:, 256:])
    for r in range(16):
        out[xh, r] = mine
        out[1 - xh, r] = other


def open_act_kernel(w, high, low):
    for e in range(0, 32, 4):
        blocks = [opened(w[e + i], 32) for i in range(4)]
        for p in range(2):
            x = jnp.concatenate([b[p] for b in blocks], axis=0).T
            top = x.astype(BF16)
            high[p, :, 32 * e:32 * e + 128] = top
            low[p, :, 32 * e:32 * e + 128] = (x - top.astype(F32)).astype(BF16)


def correct_kernel(where, act_high, act_low, *rest):
    grads, (q_out, o_out, high, low, acc, total) = rest[:5], rest[5:]
    zl, xh = lax.rem(where[0], 2), where[1]
    for side in range(2):
        half = xh if side == 0 else 1 - xh
        for k in range(16):
            if side == 0:
                w = grads[k // 8][k % 8]
            else:
                w = grads[2][k] if k < 8 else grads[3 + (k - 8) // 4][k % 4]
            block = 2 * (k % 8) + (zl if k < 8 else 1 - zl)
            at = pl.multiple_of(64 * block, 64)
            [x] = opened(w, 64)
            top = x.astype(BF16)
            high[half, pl.ds(at, 64), :] = top
            low[half, pl.ds(at, 64), :] = (x - top.astype(F32)).astype(BF16)
    for seq in range(SEQS):
        first, last = where[2 + seq], where[3 + seq]
        acc[...] = jnp.zeros_like(acc)

        def chunk(k, carry, first=first, last=last):
            at = pl.multiple_of(256 * k, 256)
            token = at + lax.broadcasted_iota(jnp.int32, (1, 256), 1)
            inside = ((token >= first) & (token < last)).astype(F32).astype(BF16)
            for p in range(2):
                a_high = act_high[p, :, pl.ds(at, 256)] * inside
                a_low = act_low[p, :, pl.ds(at, 256)] * inside
                g_high, g_low = high[p, pl.ds(at, 256), :], low[p, pl.ds(at, 256), :]
                acc[p] += (
                    jnp.dot(a_high, g_high, preferred_element_type=F32)
                    + jnp.dot(a_low, g_high, preferred_element_type=F32)
                    + jnp.dot(a_high, g_low, preferred_element_type=F32)
                )
            return carry

        lax.fori_loop(first // 256, (last + 255) // 256, chunk, 0)
        square = acc[...] * acc[...]
        total[...] = square if seq == 0 else total[...] + square
    q_out[...] = total[0].T * (1.0 / SEQS)
    o_out[...] = total[1].T * (1.0 / SEQS)


def shape(*dims, dtype=S16):
    return jax.ShapeDtypeStruct(dims, dtype)


def per_device(seq_ids, qx, qg, qa, qb, ox, og, oa, ob):
    z = lax.axis_index(Z)
    xh = lax.axis_index("xh")
    bounds = jnp.sum(
        (seq_ids[None, :] < jnp.arange(SEQS + 1, dtype=jnp.int32)[:, None]).astype(jnp.int32), axis=1
    )
    where = jnp.concatenate([jnp.stack([z, xh]).astype(jnp.int32), bounds, jnp.zeros(1, jnp.int32)])

    grads = jnp.stack([qg, og])
    sent = jnp.broadcast_to(grads[:, None], (2, 16, 64, 256)).reshape(32, 64, 256)
    got = lax.all_to_all(sent, PLANE, split_axis=0, concat_axis=0, tiled=True)
    got = got.reshape(2, 16, 64, 256)
    grad_other = swap_half(jnp.where(xh == 0, ob, qb))
    level = lax.all_gather(jnp.stack([qx, ox])[None], ZH, axis=0, tiled=True)

    keep, *sends = whole(
        rotate_grad_kernel,
        [shape(4, 64, 512, dtype=F32)] + [shape(4, 72, 512)] * 2 + [shape(2, 72, 512)] * 2,
        [where, got, qb, ob, grad_other],
        flops=2 * 2 * 512 * 512 * 512,
    )
    *sends, qa, oa, level = lax.optimization_barrier((*sends, qa, oa, level))
    ups = [shift(w, by) for w, by in zip(sends[2:], (2, -2))]
    sends = [shift(w, by) for w, by in zip(sends[:2], (1, -1))] + ups
    act_other = swap_half(jnp.stack([qa, oa]))
    [words] = whole(near_sum_kernel, [shape(4, 72, 512)], [keep] + sends, scalars=0)
    words, level = lax.optimization_barrier((words, level))
    inputs = [level] + [
        shift(w, by) for w, by in ((level, 1), (level, -1), (level[:2], 2), (level[2:], -2))
    ]
    words = lax.all_to_all(words, ZH, split_axis=0, concat_axis=0, tiled=True)
    [words] = whole(far_sum_kernel, [shape(1, 72, 512)], [words], scalars=0)

    [act_words] = whole(
        rotate_act_kernel,
        [shape(16, 72, 512)],
        [where] + inputs + [qa, oa, act_other],
        flops=2 * 2 * 512 * 512 * 512,
    )
    words, act_words = lax.optimization_barrier((words, act_words))
    act_words = lax.all_to_all(act_words, ROW, split_axis=0, concat_axis=0, tiled=True)

    words = lax.all_gather(words, Z8, axis=0, tiled=True)
    other = swap_half(words)
    words, act_words = lax.optimization_barrier((words, act_words))
    words, other = lax.optimization_barrier((words, other))
    mine = [words, lax.ppermute(words, "zl", [(0, 1), (1, 0)])]
    others = [other, shift(other[:4], 1), shift(other[4:], -1)]

    [act_words] = whole(act_sum_kernel, [shape(2, 16, 72, 256)], [where, act_words])
    act_words = act_words.reshape(32, 72, 256)
    act_words = lax.all_to_all(act_words, PLANE, split_axis=0, concat_axis=0, tiled=True)
    act = whole(open_act_kernel, [shape(2, 256, 1024, dtype=BF16)] * 2, [act_words], scalars=0)

    return tuple(
        whole(
            correct_kernel,
            [shape(512, 256, dtype=F32)] * 2,
            [where] + list(act) + mine + others,
            scratch=[
                pltpu.VMEM((2, 1024, 512), BF16),
                pltpu.VMEM((2, 1024, 512), BF16),
                pltpu.VMEM((2, 256, 512), F32),
                pltpu.VMEM((2, 256, 512), F32),
            ],
            flops=2 * 2 * 7 * 3 * 256 * 512 * 256,
        )
    )


def solution(mesh):
    fine = Mesh(mesh.devices.reshape(2, 4, 2, 2, 4, 2, 2), ("xl", "y", "c", "xh") + Z)
    row, col = ROW, ("xh",) + Z
    one = (P(col, row), P(row, col), P(row, col), P(col, row))
    out_specs = (P(row, col), P(row, col))
    return jax.shard_map(
        per_device, mesh=fine, in_specs=(P(),) + one + one, out_specs=out_specs, check_vma=False
    )
```
